32 devices in a mesh: aux: 4 (over z), ao: 8 (over y, x, core).
Axes of the slice: x: 2, y: 2, z: 4, core: 2. Of those that a mesh axis runs over, the one named last changes fastest.
Arguments:
- soc_ints: bfloat16 [512, 3, 16, 8192], P('aux', None, None, 'ao'), may hold values from -6 to 6
- cou_ints: bfloat16 [512, 16, 8192], P('aux', None, 'ao'), may hold values from -6 to 6
- coef_t: bfloat16 [16, 8192], P(None, 'ao'), may hold values from -0.0625 to 0.0625
- active_rdm: float32 [16, 16], replicated, may hold values from -3 to 3
- spin_dens: bfloat16 [80, 256], P('ao'), may hold values from -6 to 6
- pair_list: int32 [80, 2], replicated, may hold values from 0 to 23
- owner_map: int32 [80], P('ao'), may hold values from 0 to 79, each once
- state_count: int32 [24], replicated, may hold values from 8 to 16, as said below
Outputs:
- soc_elems: float32 [3, 80], P(None, 'ao')
The draws below stay inside these ranges and needn't reach their ends.
Inputs may be any that keep to these rules, and one draw needn't show every extreme that they name: `state_count`: each state's count of live active orbitals; some state has all 16. `owner_map`: every pair appears in exactly one slot.
All inputs are finite; a program needn't handle non-finite values.
Results may differ from the reference program's by a relative error of at most 0.0003.
Values may be sent and summed in bfloat16 or wider, within the bound.
A program may use at most 64 MiB of HBM per device.

```python
import jax
import jax.numpy as jnp
from jax import lax

NAO = 8192
NACT = 16
NSTATE = 24
NAUX = 512
NPAIR = 80


def draw_state_count(key, part):
    counts = jax.random.randint(jax.random.fold_in(key, 11), (NSTATE,), NACT // 2, NACT + 1)
    chosen = jax.random.randint(jax.random.fold_in(key, 12), (), 0, NSTATE)
    return jnp.where(jnp.arange(NSTATE) == chosen, NACT, counts).astype(jnp.int32)


def plant(array, key, least, largest):
    place = [jax.random.randint(jax.random.fold_in(key, axis), (), 0, length) for axis, length in enumerate(array.shape)]
    main_axis = array.shape.index(max(array.shape))
    next_to = place[:main_axis] + [(place[main_axis] + 1) % array.shape[main_axis]] + place[main_axis + 1:]
    return array.at[tuple(place)].set(least).at[tuple(next_to)].set(largest)


def level_of(stream_key, dims, shards, least, largest):
    def one(dim, shards_of):
        heights = jax.random.uniform(jax.random.fold_in(jax.random.fold_in(stream_key, 6), dim), (shards_of,), jnp.float32, least / len(shards), largest / len(shards))
        return jnp.repeat(jnp.exp(heights), dims[dim] // shards_of).reshape((-1,) + (1,) * (len(dims) - dim - 1))

    level = one(*shards[0])
    for cut in shards[1:]:
        level = level * one(*cut)
    return level


def scatter_about(stream_key, shape, scale, most, cuts=(), kind=jnp.bfloat16):
    array = jax.random.normal(stream_key, shape, jnp.float32) * scale
    if len(cuts) > 0:
        array = level_of(stream_key, shape, cuts, -0.22, 0.18) * array
    return jnp.clip(array, min=-most, max=most).astype(kind)


def setup_inputs(seed: int = 0) -> dict:
    seeds = jax.random.split(jax.random.key(seed), 9)
    soc_ints = scatter_about(seeds[0], (NAUX, 3, NACT, NAO), 1.0, 6.0, ((0, 4), (3, 8)))
    cou_ints = scatter_about(seeds[1], (NAUX, NACT, NAO), 1.0, 6.0, ((0, 4), (2, 8)))
    coef_t = scatter_about(seeds[2], (NACT, NAO), NAO ** -0.5, 0.0625, ((1, 8),))
    active_rdm = scatter_about(seeds[3], (NACT, NACT), 0.5, 3.0, (), jnp.float32)
    spin_dens = scatter_about(seeds[4], (NPAIR, NACT * NACT), 1.0, 6.0, ((0, 8),))
    pair_list = plant(jax.random.randint(seeds[5], (NPAIR, 2), 0, NSTATE), jax.random.fold_in(seeds[5], 1), 0, NSTATE - 1).astype(jnp.int32)
    owner_map = jax.random.permutation(seeds[6], NPAIR).astype(jnp.int32)
    state_count = draw_state_count(jax.random.fold_in(seeds[8], 71), 0)
    return dict(soc_ints=soc_ints, cou_ints=cou_ints, coef_t=coef_t, active_rdm=active_rdm, spin_dens=spin_dens, pair_list=pair_list, owner_map=owner_map, state_count=state_count)


def mean_field(soc_rows, cou_rows, active_rdm, scale):
    count = soc_rows.shape[0]
    width = active_rdm.shape[0]
    high = lax.Precision.HIGHEST
    fitted = jnp.dot(cou_rows, active_rdm.reshape(-1), precision=high)
    direct = jnp.einsum('p,pxk->xk', fitted, soc_rows, precision=high)
    folded = jnp.einsum('vw,pwu->pvu', active_rdm, cou_rows.reshape(count, width, width), precision=high)
    crossed = jnp.einsum('pxtv,pvu->xtu', soc_rows.reshape(count, 3, width, width), folded, precision=high)
    return (direct - 1.5 * crossed.reshape(3, width * width)) * scale

def reference(soc_ints, cou_ints, coef_t, active_rdm, spin_dens, pair_list, owner_map, state_count):
    width = NACT
    cells = width * width
    soc_mo = jnp.dot(soc_ints.reshape(-1, NAO), coef_t.T, preferred_element_type=jnp.float32).reshape(NAUX, 3, cells)
    cou_mo = jnp.dot(cou_ints.reshape(-1, NAO), coef_t.T, preferred_element_type=jnp.float32).reshape(NAUX, cells)
    scale = 1.0 / (8.0 * jnp.sqrt(jnp.float32(NAUX)))
    field = mean_field(soc_mo, cou_mo, active_rdm, scale)
    bra_count = state_count[pair_list[:, 0]]
    ket_count = state_count[pair_list[:, 1]]
    live = jnp.minimum(bra_count, ket_count)
    cell = jnp.arange(cells, dtype=jnp.int32)
    inside = (cell[None, :] // width < live[:, None]) & (cell[None, :] % width < live[:, None])
    dens = jnp.where(inside, spin_dens.astype(jnp.float32), jnp.float32(0.0))
    pair_val = jnp.dot(field, dens.T, precision=lax.Precision.HIGHEST) / width
    return jnp.take(pair_val, owner_map, axis=1)
```

```python
import functools

import jax
import jax.numpy as jnp
from jax import lax
from jax.experimental import pallas as pl
from jax.experimental.pallas import tpu as pltpu
from jax.sharding import PartitionSpec as P

MESH = pl.DeviceIdType.MESH
HIGH = lax.Precision.HIGHEST
NN = (((1,), (0,)), ((), ()))
NT = (((1,), (1,)), ((), ()))


def iota(shape, dim):
    return lax.broadcasted_iota(jnp.int32, shape, dim)


def dot(a, b, dims):
    return lax.dot_general(a, b, dims, precision=HIGH, preferred_element_type=jnp.float32)


def kernel(
    n, m, chunks, k, scale,
    soc_ref, cou_ref, coef_ref, rdm_ref, dens_ref, pair_ref, owner_ref, count_ref,
    out_ref,
    soc_v, cou_v, send, recv, dens_out, dens_all, dmat, fit_w, fold_w,
    part_a, part_b,
    soc_sem, cou_sem, send_sem, recv_sem, dsend_sem, drecv_sem,
    asend_sem, arecv_sem, bsend_sem, brecv_sem,
):
    width = rdm_ref.shape[0]
    own = dens_ref.shape[0]
    cells = width * width
    states = count_ref.shape[1]
    pairs = pair_ref.shape[1]
    rows_p = n * 16
    me = lax.axis_index("ao")
    z = lax.axis_index("aux")

    def peer(d):
        return lax.rem(me + 1 + d, n)

    def fetch(c, d):
        at = (c * n + peer(d)) * k
        return (
            pltpu.make_async_copy(soc_ref.at[pl.ds(at, k)], soc_v.at[pl.ds(at, k)], soc_sem.at[c, d]),
            pltpu.make_async_copy(cou_ref.at[pl.ds(at, k)], cou_v.at[pl.ds(at, k)], cou_sem.at[c, d]),
        )

    def start_fetch(i, carry):
        for copy in fetch(i // n, lax.rem(i, n)):
            copy.start()
        return carry

    lax.fori_loop(0, n, start_fetch, 0)

    barrier = pltpu.get_barrier_semaphore()
    for d in range(n - 1):
        pl.semaphore_signal(barrier, inc=1, device_id=(z, peer(d)), device_id_type=MESH)
    for d in range(m - 1):
        pl.semaphore_signal(
            barrier, inc=1, device_id=(lax.rem(z + 1 + d, m), me), device_id_type=MESH
        )

    lax.fori_loop(n, chunks * n, start_fetch, 0)

    dens = dens_ref[...].astype(jnp.float32)
    if own < 16:
        dens = jnp.concatenate([dens, jnp.zeros((16 - own, cells), jnp.float32)], axis=0)
    dens_out[...] = dens.astype(jnp.bfloat16)
    dens_all[me] = dens.astype(jnp.bfloat16)

    pl.semaphore_wait(barrier, n + m - 2)

    def dens_copy(d):
        return pltpu.make_async_remote_copy(
            src_ref=dens_out, dst_ref=dens_all.at[me], send_sem=dsend_sem, recv_sem=drecv_sem,
            device_id=(z, peer(d)), device_id_type=MESH,
        )

    def block_copy(c, d):
        j = peer(d)
        return pltpu.make_async_remote_copy(
            src_ref=send.at[c, j], dst_ref=recv.at[c, me],
            send_sem=send_sem.at[c], recv_sem=recv_sem.at[c],
            device_id=(z, j), device_id_type=MESH,
        )

    def transform(c, d):
        for copy in fetch(c, d):
            copy.wait()
        at = (c * n + peer(d)) * k
        span = soc_v.shape[-1]
        rows = jnp.concatenate(
            [
                soc_v[pl.ds(at, k)].reshape(3 * width * k, span),
                cou_v[pl.ds(at, k)].reshape(width * k, span),
            ],
            axis=0,
        )
        return lax.dot_general(coef_ref[...], rows, NT, preferred_element_type=jnp.float32)

    for d in range(n - 1):
        dens_copy(d).start()

    lanes = width * k
    rdm = rdm_ref[...]
    spread = (lax.rem(iota((width, lanes), 1), width) == iota((width, lanes), 0)).astype(jnp.float32)
    tiled = jnp.concatenate([rdm] * k, axis=0)
    eye = (iota((width, width), 0) == iota((width, width), 1)).astype(jnp.float32)
    fit_w[...] = dot(eye, tiled, NT)
    wide = dot(rdm, spread, NN)
    wide = jnp.concatenate([wide] * k, axis=0)
    same = iota((lanes, lanes), 0) // width == iota((lanes, lanes), 1) // width
    fold_w[...] = jnp.where(same, -1.5 * wide, 0.0)

    def chunk(c, carry):
        def one(d, carry):
            send[c, peer(d)] = transform(c, d)
            block_copy(c, d).start()
            return carry

        lax.fori_loop(0, n - 1, one, 0)
        recv[c, me] = transform(c, n - 1)
        return carry

    lax.fori_loop(0, chunks, chunk, 0)

    pltpu.make_async_copy(
        dens_all.at[pl.ds(0, n - 1)], dens_all.at[pl.ds(0, n - 1)], drecv_sem
    ).wait()
    bra = iota((states, pairs), 0) == pair_ref[0:1, :]
    ket = iota((states, pairs), 0) == pair_ref[1:2, :]
    counts = jnp.broadcast_to(count_ref[...].astype(jnp.float32), (8, states))
    bra_count = dot(counts, bra.astype(jnp.float32), NN)
    ket_count = dot(counts, ket.astype(jnp.float32), NN)
    live_row = jnp.minimum(bra_count, ket_count)[0:1, :]
    row = iota((rows_p, pairs), 0)
    place = (lax.rem(row, 16) < own) & (row // 16 * own + lax.rem(row, 16) == iota((rows_p, pairs), 1))
    live = jnp.sum(jnp.where(place, live_row, 0.0), axis=1, keepdims=True).astype(jnp.int32)
    cell = iota((rows_p, cells), 1)
    inside = (cell // width < live) & (lax.rem(cell, width) < live)
    dmat[...] = jnp.where(inside, dens_all[...].astype(jnp.float32).reshape(rows_p, cells), 0.0)

    total = []
    for c in range(chunks):
        block = recv.at[c, pl.ds(0, n - 1)]
        pltpu.make_async_copy(block, block, recv_sem.at[c]).wait()
        summed = recv[c, 0]
        for s in range(1, n):
            summed = summed + recv[c, s]
        total.append(summed)

    cou_t = jnp.concatenate([t[:, 3 * lanes:] for t in total], axis=0)
    fit_in = cou_t * jnp.concatenate([fit_w[...]] * chunks, axis=0)
    fit_in = jnp.broadcast_to(
        jnp.sum(fit_in.reshape(chunks, width, lanes), axis=1, keepdims=True), (chunks, width, lanes)
    ).reshape(chunks * width, lanes)
    fitted = dot(fit_in, same.astype(jnp.float32), NN)
    down = iota((chunks * width, lanes), 0)
    across = iota((chunks * width, lanes), 1)
    diagonal = lax.rem(down, width) == lax.rem(across, width)
    mixed = dot(cou_t, fold_w[...], NT) + jnp.where(diagonal, fitted, 0.0)
    field = None
    for c in range(chunks):
        stacked = jnp.concatenate(
            [total[c][:, 3 * width * p: 3 * width * (p + 1)] for p in range(k)], axis=0
        )
        term = dot(mixed[c * width:(c + 1) * width], stacked, NN)
        field = term if field is None else field + term
    field = field * scale

    deep = 3 * width
    keep = iota((cells, deep), 0) // width == lax.rem(iota((cells, deep), 1), width)
    laid = jnp.where(keep, jnp.concatenate([field] * width, axis=0), 0.0)
    pick = (iota((8, deep), 1) // width == iota((8, deep), 0)).astype(jnp.float32)
    flat = dot(pick, laid, NT)
    value = dot(flat, dmat[...], NT)

    part_a[me] = value

    def a_copy(d):
        return pltpu.make_async_remote_copy(
            src_ref=part_a.at[me], dst_ref=part_a.at[me], send_sem=asend_sem, recv_sem=arecv_sem,
            device_id=(z, peer(d)), device_id_type=MESH,
        )

    for d in range(n - 1):
        a_copy(d).start()
    block = part_a.at[pl.ds(0, n - 1)]
    pltpu.make_async_copy(block, block, arecv_sem).wait()
    value = part_a[0]
    for s in range(1, n):
        value = value + part_a[s]

    part_b[z] = value

    def b_copy(d):
        return pltpu.make_async_remote_copy(
            src_ref=part_b.at[z], dst_ref=part_b.at[z], send_sem=bsend_sem, recv_sem=brecv_sem,
            device_id=(lax.rem(z + 1 + d, m), me), device_id_type=MESH,
        )

    for d in range(m - 1):
        b_copy(d).start()
    block = part_b.at[pl.ds(0, m - 1)]
    pltpu.make_async_copy(block, block, brecv_sem).wait()
    value = part_b[0]
    for s in range(1, m):
        value = value + part_b[s]

    slots = owner_ref.shape[1]
    row = iota((rows_p, slots), 0)
    chosen = (lax.rem(row, 16) < own) & (row // 16 * own + lax.rem(row, 16) == owner_ref[...])
    out_ref[...] = dot(value, chosen.astype(jnp.float32), NN)[0:3, :]

    pltpu.make_async_copy(
        dens_all.at[pl.ds(0, n - 1)], dens_all.at[pl.ds(0, n - 1)], dsend_sem
    ).wait()
    for c in range(chunks):
        block = send.at[c, pl.ds(0, n - 1)]
        pltpu.make_async_copy(block, block, send_sem.at[c]).wait()
    block = part_a.at[pl.ds(0, n - 1)]
    pltpu.make_async_copy(block, block, asend_sem).wait()
    block = part_b.at[pl.ds(0, m - 1)]
    pltpu.make_async_copy(block, block, bsend_sem).wait()


def on_device(n, m, soc_ints, cou_ints, coef_t, active_rdm, spin_dens, pair_list, owner_map, state_count):
    slab, parts, width, span = soc_ints.shape
    k = max(1, slab // (n * 4))
    chunks = slab // (n * k)
    block = (parts + 1) * width * k
    own, cells = spin_dens.shape
    rows_p = n * 16
    scale = 1.0 / (8.0 * float(slab * m) ** 0.5 * width)
    vmem = pl.BlockSpec(memory_space=pltpu.VMEM)
    hbm = pl.BlockSpec(memory_space=pl.ANY)
    dma = pltpu.SemaphoreType.DMA
    return pl.pallas_call(
        functools.partial(kernel, n, m, chunks, k, scale),
        out_shape=jax.ShapeDtypeStruct((parts, owner_map.shape[0]), jnp.float32),
        in_specs=[hbm, hbm] + [vmem] * 6,
        out_specs=vmem,
        scratch_shapes=[
            pltpu.VMEM((slab, parts * width, span), jnp.bfloat16),
            pltpu.VMEM((slab, width, span), jnp.bfloat16),
            pltpu.VMEM((chunks, n, width, block), jnp.float32),
            pltpu.VMEM((chunks, n, width, block), jnp.float32),
            pltpu.VMEM((16, cells), jnp.bfloat16),
            pltpu.VMEM((n, 16, cells), jnp.bfloat16),
            pltpu.VMEM((rows_p, cells), jnp.float32),
            pltpu.VMEM((width, width * k), jnp.float32),
            pltpu.VMEM((width * k, width * k), jnp.float32),
            pltpu.VMEM((n, 8, rows_p), jnp.float32),
            pltpu.VMEM((m, 8, rows_p), jnp.float32),
            dma((chunks, n)), dma((chunks, n)), dma((chunks,)), dma((chunks,)),
            dma, dma, dma, dma, dma, dma,
        ],
        compiler_params=pltpu.CompilerParams(
            collective_id=0, has_side_effects=True, vmem_limit_bytes=60 * 1024 * 1024
        ),
        cost_estimate=pl.CostEstimate(
            flops=2 * slab * 4 * width * width * span, bytes_accessed=slab * 4 * width * span * 2,
            transcendentals=0,
        ),
    )(
        soc_ints.reshape(slab, parts * width, span), cou_ints, coef_t, active_rdm, spin_dens,
        pair_list.T, owner_map.reshape(1, -1), state_count.reshape(1, -1),
    )


def solution(mesh):
    return jax.shard_map(
        functools.partial(on_device, mesh.shape["ao"], mesh.shape["aux"]),
        mesh=mesh,
        in_specs=(
            P("aux", None, None, "ao"),
            P("aux", None, "ao"),
            P(None, "ao"),
            P(),
            P("ao", None),
            P(),
            P("ao"),
            P(),
        ),
        out_specs=P(None, "ao"),
        check_vma=False,
    )
```

```python
import functools

import jax
import jax.numpy as jnp
from jax import lax
from jax.experimental import pallas as pl
from jax.experimental.pallas import tpu as pltpu
from jax.sharding import PartitionSpec as P

MESH = pl.DeviceIdType.MESH
HIGH = lax.Precision.HIGHEST
NN = (((1,), (0,)), ((), ()))
NT = (((1,), (1,)), ((), ()))


def iota(shape, dim):
    return lax.broadcasted_iota(jnp.int32, shape, dim)


def dot(a, b, dims):
    return lax.dot_general(a, b, dims, precision=HIGH, preferred_element_type=jnp.float32)


def parts_of(x):
    hi = x.astype(jnp.bfloat16)
    rest = x - hi.astype(jnp.float32)
    mid = rest.astype(jnp.bfloat16)
    return hi, mid, (rest - mid.astype(jnp.float32)).astype(jnp.bfloat16)


def exact_dot(x, table, dims):
    rows = x.shape[0]
    stack = jnp.concatenate([p.astype(jnp.float32) for p in parts_of(x)], axis=0).astype(jnp.bfloat16)
    out = lax.dot_general(stack, table.astype(jnp.bfloat16), dims, preferred_element_type=jnp.float32)
    return out[:rows] + out[rows:2 * rows] + out[2 * rows:3 * rows]


def kernel(
    n, m, chunks, k, group, scale,
    soc_ref, cou_ref, coef_hbm, rdm_hbm, dens_hbm, pair_hbm, owner_hbm, count_hbm,
    out_ref,
    coef_ref, rdm_ref, dens_ref, pair_ref, owner_ref, count_ref, small_sem,
    soc_v, cou_v, send, recv, dens_out, dens_all, dmat, fit_w, fold_w,
    part_a, part_b,
    soc_sem, cou_sem, send_sem, recv_sem, dsend_sem, drecv_sem,
    asend_sem, arecv_sem, bsend_sem, brecv_sem,
):
    width = rdm_ref.shape[0]
    own = dens_ref.shape[0]
    cells = width * width
    states = count_ref.shape[1]
    pairs = pair_ref.shape[1]
    rows_p = n * 16
    me = lax.axis_index("ao")
    z = lax.axis_index("aux")

    def peer(d):
        chip = lax.rem(me // 2 + 1 + d // 2, n // 2)
        return chip * 2 + lax.rem(me + 1 + d, 2)

    def fetch(c, d):
        at = (c * n + peer(d)) * k
        return (
            pltpu.make_async_copy(soc_ref.at[pl.ds(at, k)], soc_v.at[pl.ds(at, k)], soc_sem.at[c, d]),
            pltpu.make_async_copy(cou_ref.at[pl.ds(at, k)], cou_v.at[pl.ds(at, k)], cou_sem.at[c, d]),
        )

    def start_fetch(i, carry):
        for copy in fetch(i // n, lax.rem(i, n)):
            copy.start()
        return carry

    lax.fori_loop(0, group, start_fetch, 0)
    small = [
        pltpu.make_async_copy(a, b, small_sem.at[i])
        for i, (a, b) in enumerate([
            (coef_hbm, coef_ref), (rdm_hbm, rdm_ref), (dens_hbm, dens_ref),
            (pair_hbm, pair_ref), (owner_hbm, owner_ref), (count_hbm, count_ref),
        ])
    ]
    for copy in small:
        copy.start()

    barrier = pltpu.get_barrier_semaphore()
    for d in range(n - 1):
        pl.semaphore_signal(barrier, inc=1, device_id=(z, peer(d)), device_id_type=MESH)
    for d in range(m - 1):
        pl.semaphore_signal(
            barrier, inc=1, device_id=(lax.rem(z + 1 + d, m), me), device_id_type=MESH
        )

    lax.fori_loop(group, chunks * n, start_fetch, 0)
    for copy in small:
        copy.wait()

    dens = dens_ref[...].astype(jnp.float32)
    if own < 16:
        dens = jnp.concatenate([dens, jnp.zeros((16 - own, cells), jnp.float32)], axis=0)
    dens_out[...] = dens.astype(jnp.bfloat16)
    dens_all[me] = dens.astype(jnp.bfloat16)

    pl.semaphore_wait(barrier, n + m - 2)

    def dens_copy(d):
        return pltpu.make_async_remote_copy(
            src_ref=dens_out, dst_ref=dens_all.at[me], send_sem=dsend_sem, recv_sem=drecv_sem,
            device_id=(z, peer(d)), device_id_type=MESH,
        )

    def block_copy(c, d):
        j = peer(d)
        return pltpu.make_async_remote_copy(
            src_ref=send.at[c, j], dst_ref=recv.at[c, me],
            send_sem=send_sem.at[c], recv_sem=recv_sem.at[c],
            device_id=(z, j), device_id_type=MESH,
        )

    span = soc_v.shape[-1]
    block_rows = 4 * width * k

    def transform(c, first):
        for i in range(group):
            for copy in fetch(c, first + i):
                copy.wait()
        rows = []
        for i in range(group):
            at = (c * n + peer(first + i)) * k
            rows.append(soc_v[pl.ds(at, k)].reshape(3 * width * k, span))
            rows.append(cou_v[pl.ds(at, k)].reshape(width * k, span))
        out = lax.dot_general(
            coef_ref[...], jnp.concatenate(rows, axis=0), NT, preferred_element_type=jnp.float32
        )
        return [out[:, i * block_rows:(i + 1) * block_rows] for i in range(group)]

    for d in range(n - 1):
        dens_copy(d).start()

    lanes = width * k
    rdm = rdm_ref[...]
    spread = (lax.rem(iota((width, lanes), 1), width) == iota((width, lanes), 0)).astype(jnp.float32)
    tiled = jnp.concatenate([rdm] * k, axis=0)
    eye = (iota((width, width), 0) == iota((width, width), 1)).astype(jnp.float32)
    fit_w[...] = dot(eye, tiled, NT)
    wide = dot(rdm, spread, NN)
    wide = jnp.concatenate([wide] * k, axis=0)
    same = iota((lanes, lanes), 0) // width == iota((lanes, lanes), 1) // width
    fold_w[...] = jnp.where(same, -1.5 * wide, 0.0)

    def chunk(c, carry):
        def one(g, carry):
            for i, block in enumerate(transform(c, g * group)):
                send[c, peer(g * group + i)] = block
                block_copy(c, g * group + i).start()
            return carry

        lax.fori_loop(0, n // group - 1, one, 0)
        last = n - group
        for i, block in enumerate(transform(c, last)):
            if i < group - 1:
                send[c, peer(last + i)] = block
                block_copy(c, last + i).start()
            else:
                recv[c, me] = block
        return carry

    lax.fori_loop(0, chunks, chunk, 0)

    pltpu.make_async_copy(
        dens_all.at[pl.ds(0, n - 1)], dens_all.at[pl.ds(0, n - 1)], drecv_sem
    ).wait()
    bra = iota((states, pairs), 0) == pair_ref[0:1, :]
    ket = iota((states, pairs), 0) == pair_ref[1:2, :]
    counts = jnp.broadcast_to(count_ref[...].astype(jnp.float32), (8, states)).astype(jnp.bfloat16)
    bra_count = lax.dot_general(
        counts, bra.astype(jnp.float32).astype(jnp.bfloat16), NN, preferred_element_type=jnp.float32
    )
    ket_count = lax.dot_general(
        counts, ket.astype(jnp.float32).astype(jnp.bfloat16), NN, preferred_element_type=jnp.float32
    )
    live_row = jnp.minimum(bra_count, ket_count)[0:1, :]
    row = iota((rows_p, pairs), 0)
    place = (lax.rem(row, 16) < own) & (row // 16 * own + lax.rem(row, 16) == iota((rows_p, pairs), 1))
    live = jnp.sum(jnp.where(place, live_row, 0.0), axis=1, keepdims=True).astype(jnp.int32)
    cell = iota((rows_p, cells), 1)
    inside = (cell // width < live) & (lax.rem(cell, width) < live)
    dmat[...] = jnp.where(inside, dens_all[...].astype(jnp.float32).reshape(rows_p, cells), 0.0)

    total = []
    for c in range(chunks):
        block = recv.at[c, pl.ds(0, n - 1)]
        pltpu.make_async_copy(block, block, recv_sem.at[c]).wait()
        summed = recv[c, 0]
        for s in range(1, n):
            summed = summed + recv[c, s]
        total.append(summed)

    cou_t = jnp.concatenate([t[:, 3 * lanes:] for t in total], axis=0)
    fit_in = cou_t * jnp.concatenate([fit_w[...]] * chunks, axis=0)
    fit_in = jnp.broadcast_to(
        jnp.sum(fit_in.reshape(chunks, width, lanes), axis=1, keepdims=True), (chunks, width, lanes)
    ).reshape(chunks * width, lanes)
    fitted = exact_dot(fit_in, same.astype(jnp.float32), NN)
    down = iota((chunks * width, lanes), 0)
    across = iota((chunks * width, lanes), 1)
    diagonal = lax.rem(down, width) == lax.rem(across, width)
    mixed = dot(cou_t, fold_w[...], NT) + jnp.where(diagonal, fitted, 0.0)
    stacked = jnp.concatenate(
        [t[:, 3 * width * p: 3 * width * (p + 1)] for t in total for p in range(k)], axis=0
    )
    mixed = jnp.concatenate([mixed[c * width:(c + 1) * width] for c in range(chunks)], axis=1)
    field = dot(mixed, stacked, NN) * scale

    deep = 3 * width
    laid = jnp.concatenate([p.astype(jnp.float32) for p in parts_of(field)], axis=1)
    laid = jnp.concatenate([laid] * width, axis=0)
    keep = iota((cells, 3 * deep), 0) // width == lax.rem(iota((cells, 3 * deep), 1), width)
    laid = jnp.where(keep, laid, 0.0).astype(jnp.bfloat16)
    pick = lax.rem(iota((8, 3 * deep), 1), deep) // width == iota((8, 3 * deep), 0)
    flat = lax.dot_general(
        pick.astype(jnp.float32).astype(jnp.bfloat16), laid, NT, preferred_element_type=jnp.float32
    )
    value = exact_dot(flat, dmat[...], NT)

    part_a[me] = value

    def a_copy(d):
        return pltpu.make_async_remote_copy(
            src_ref=part_a.at[me], dst_ref=part_a.at[me], send_sem=asend_sem, recv_sem=arecv_sem,
            device_id=(z, peer(d)), device_id_type=MESH,
        )

    for d in range(n - 1):
        a_copy(d).start()
    block = part_a.at[pl.ds(0, n - 1)]
    pltpu.make_async_copy(block, block, arecv_sem).wait()
    value = part_a[0]
    for s in range(1, n):
        value = value + part_a[s]

    part_b[z] = value

    def b_copy(d):
        return pltpu.make_async_remote_copy(
            src_ref=part_b.at[z], dst_ref=part_b.at[z], send_sem=bsend_sem, recv_sem=brecv_sem,
            device_id=(lax.rem(z + 1 + d, m), me), device_id_type=MESH,
        )

    for d in range(m - 1):
        b_copy(d).start()
    block = part_b.at[pl.ds(0, m - 1)]
    pltpu.make_async_copy(block, block, brecv_sem).wait()
    value = part_b[0]
    for s in range(1, m):
        value = value + part_b[s]

    slots = owner_ref.shape[1]
    row = iota((rows_p, slots), 0)
    chosen = (lax.rem(row, 16) < own) & (row // 16 * own + lax.rem(row, 16) == owner_ref[...])
    out_ref[...] = exact_dot(value, chosen.astype(jnp.float32), NN)[0:3, :]

    pltpu.make_async_copy(
        dens_all.at[pl.ds(0, n - 1)], dens_all.at[pl.ds(0, n - 1)], dsend_sem
    ).wait()
    for c in range(chunks):
        block = send.at[c, pl.ds(0, n - 1)]
        pltpu.make_async_copy(block, block, send_sem.at[c]).wait()
    block = part_a.at[pl.ds(0, n - 1)]
    pltpu.make_async_copy(block, block, asend_sem).wait()
    block = part_b.at[pl.ds(0, m - 1)]
    pltpu.make_async_copy(block, block, bsend_sem).wait()


def on_device(n, m, soc_ints, cou_ints, coef_t, active_rdm, spin_dens, pair_list, owner_map, state_count):
    slab, parts, width, span = soc_ints.shape
    k = max(1, slab // (n * 4))
    chunks = slab // (n * k)
    block = (parts + 1) * width * k
    own, cells = spin_dens.shape
    rows_p = n * 16
    scale = 1.0 / (8.0 * float(slab * m) ** 0.5 * width)
    vmem = pl.BlockSpec(memory_space=pltpu.VMEM)
    hbm = pl.BlockSpec(memory_space=pl.ANY)
    dma = pltpu.SemaphoreType.DMA
    return pl.pallas_call(
        functools.partial(kernel, n, m, chunks, k, 4, scale),
        out_shape=jax.ShapeDtypeStruct((parts, owner_map.shape[0]), jnp.float32),
        in_specs=[hbm] * 8,
        out_specs=vmem,
        scratch_shapes=[
            pltpu.VMEM((width, span), jnp.bfloat16),
            pltpu.VMEM((width, width), jnp.float32),
            pltpu.VMEM((own, cells), jnp.bfloat16),
            pltpu.VMEM((2, pair_list.shape[0]), jnp.int32),
            pltpu.VMEM((1, own), jnp.int32),
            pltpu.VMEM((1, state_count.shape[0]), jnp.int32),
            dma((6,)),
            pltpu.VMEM((slab, parts * width, span), jnp.bfloat16),
            pltpu.VMEM((slab, width, span), jnp.bfloat16),
            pltpu.VMEM((chunks, n, width, block), jnp.float32),
            pltpu.VMEM((chunks, n, width, block), jnp.float32),
            pltpu.VMEM((16, cells), jnp.bfloat16),
            pltpu.VMEM((n, 16, cells), jnp.bfloat16),
            pltpu.VMEM((rows_p, cells), jnp.float32),
            pltpu.VMEM((width, width * k), jnp.float32),
            pltpu.VMEM((width * k, width * k), jnp.float32),
            pltpu.VMEM((n, 8, rows_p), jnp.float32),
            pltpu.VMEM((m, 8, rows_p), jnp.float32),
            dma((chunks, n)), dma((chunks, n)), dma((chunks,)), dma((chunks,)),
            dma, dma, dma, dma, dma, dma,
        ],
        compiler_params=pltpu.CompilerParams(
            collective_id=0, has_side_effects=True, vmem_limit_bytes=60 * 1024 * 1024
        ),
        cost_estimate=pl.CostEstimate(
            flops=2 * slab * 4 * width * width * span, bytes_accessed=slab * 4 * width * span * 2,
            transcendentals=0,
        ),
    )(
        soc_ints.reshape(slab, parts * width, span), cou_ints, coef_t, active_rdm, spin_dens,
        pair_list.T, owner_map.reshape(1, -1), state_count.reshape(1, -1),
    )


def solution(mesh):
    return jax.shard_map(
        functools.partial(on_device, mesh.shape["ao"], mesh.shape["aux"]),
        mesh=mesh,
        in_specs=(
            P("aux", None, None, "ao"),
            P("aux", None, "ao"),
            P(None, "ao"),
            P(),
            P("ao", None),
            P(),
            P("ao"),
            P(),
        ),
        out_specs=P(None, "ao"),
        check_vma=False,
    )
```

```python
import functools

import jax
import jax.numpy as jnp
from jax import lax
from jax.experimental import pallas as pl
from jax.experimental.pallas import tpu as pltpu
from jax.sharding import PartitionSpec as P

MESH = pl.DeviceIdType.MESH
HIGH = lax.Precision.HIGHEST
NN = (((1,), (0,)), ((), ()))
NT = (((1,), (1,)), ((), ()))


def iota(shape, dim):
    return lax.broadcasted_iota(jnp.int32, shape, dim)


def dot(a, b, dims):
    return lax.dot_general(a, b, dims, precision=HIGH, preferred_element_type=jnp.float32)


def parts_of(x):
    hi = x.astype(jnp.bfloat16)
    rest = x - hi.astype(jnp.float32)
    mid = rest.astype(jnp.bfloat16)
    return hi, mid, (rest - mid.astype(jnp.float32)).astype(jnp.bfloat16)


def exact_dot(x, table, dims):
    rows = x.shape[0]
    stack = jnp.concatenate([p.astype(jnp.float32) for p in parts_of(x)], axis=0).astype(jnp.bfloat16)
    out = lax.dot_general(stack, table.astype(jnp.bfloat16), dims, preferred_element_type=jnp.float32)
    return out[:rows] + out[rows:2 * rows] + out[2 * rows:3 * rows]


def kernel(
    n, m, chunks, k, group, scale,
    soc_ref, cou_ref, coef_hbm, rdm_hbm, dens_hbm, pair_hbm, owner_hbm, count_hbm,
    out_ref,
    coef_ref, rdm_ref, dens_ref, pair_ref, owner_ref, count_ref, small_sem,
    soc_v, cou_v, send, recv, dens_out, dens_all, dmat, fit_w, fold_w,
    part_a, part_b,
    soc_sem, cou_sem, send_sem, recv_sem, dsend_sem, drecv_sem,
    asend_sem, arecv_sem, bsend_sem, brecv_sem,
):
    width = rdm_ref.shape[0]
    own = dens_ref.shape[0]
    cells = width * width
    states = count_ref.shape[1]
    pairs = pair_ref.shape[1]
    rows_p = n * 16
    me = lax.axis_index("ao")
    z = lax.axis_index("aux")

    def peer(d):
        chip = lax.rem(me // 2 + 1 + d // 2, n // 2)
        return chip * 2 + lax.rem(me + 1 + d, 2)

    def fetch(c, d):
        at = (c * n + peer(d)) * k
        return (
            pltpu.make_async_copy(soc_ref.at[pl.ds(at, k)], soc_v.at[pl.ds(at, k)], soc_sem.at[c, d]),
            pltpu.make_async_copy(cou_ref.at[pl.ds(at, k)], cou_v.at[pl.ds(at, k)], cou_sem.at[c, d]),
        )

    def start_fetch(i, carry):
        for copy in fetch(i // n, lax.rem(i, n)):
            copy.start()
        return carry

    lax.fori_loop(0, group, start_fetch, 0)
    small = [
        pltpu.make_async_copy(a, b, small_sem.at[i])
        for i, (a, b) in enumerate([
            (coef_hbm, coef_ref), (rdm_hbm, rdm_ref), (dens_hbm, dens_ref),
            (pair_hbm, pair_ref), (owner_hbm, owner_ref), (count_hbm, count_ref),
        ])
    ]
    for copy in small:
        copy.start()

    barrier = pltpu.get_barrier_semaphore()
    for d in range(n - 1):
        pl.semaphore_signal(barrier, inc=1, device_id=(z, peer(d)), device_id_type=MESH)
    for d in range(m - 1):
        pl.semaphore_signal(
            barrier, inc=1, device_id=(lax.rem(z + 1 + d, m), me), device_id_type=MESH
        )

    lax.fori_loop(group, chunks * n, start_fetch, 0)
    for copy in small:
        copy.wait()

    dens = dens_ref[...].astype(jnp.float32)
    if own < 16:
        dens = jnp.concatenate([dens, jnp.zeros((16 - own, cells), jnp.float32)], axis=0)
    dens_out[...] = dens.astype(jnp.bfloat16)
    dens_all[me] = dens.astype(jnp.bfloat16)

    pl.semaphore_wait(barrier, n + m - 2)

    def dens_copy(d):
        return pltpu.make_async_remote_copy(
            src_ref=dens_out, dst_ref=dens_all.at[me], send_sem=dsend_sem, recv_sem=drecv_sem,
            device_id=(z, peer(d)), device_id_type=MESH,
        )

    def block_copy(c, d):
        j = peer(d)
        return pltpu.make_async_remote_copy(
            src_ref=send.at[c, j], dst_ref=recv.at[c, me],
            send_sem=send_sem.at[c], recv_sem=recv_sem.at[c],
            device_id=(z, j), device_id_type=MESH,
        )

    span = soc_v.shape[-1]
    block_rows = 4 * width * k

    def transform(c, first):
        for i in range(group):
            for copy in fetch(c, first + i):
                copy.wait()
        rows = []
        for i in range(group):
            at = (c * n + peer(first + i)) * k
            rows.append(soc_v[pl.ds(at, k)].reshape(3 * width * k, span))
            rows.append(cou_v[pl.ds(at, k)].reshape(width * k, span))
        out = lax.dot_general(
            jnp.concatenate(rows, axis=0), coef_ref[...], NT, preferred_element_type=jnp.float32
        ).T
        return [out[:, i * block_rows:(i + 1) * block_rows] for i in range(group)]

    for d in range(n - 1):
        dens_copy(d).start()

    lanes = width * k
    rdm = rdm_ref[...]
    spread = (lax.rem(iota((width, lanes), 1), width) == iota((width, lanes), 0)).astype(jnp.float32)
    tiled = jnp.concatenate([rdm] * k, axis=0)
    eye = (iota((width, width), 0) == iota((width, width), 1)).astype(jnp.float32)
    fit_w[...] = dot(eye, tiled, NT)
    wide = dot(rdm, spread, NN)
    wide = jnp.concatenate([wide] * k, axis=0)
    same = iota((lanes, lanes), 0) // width == iota((lanes, lanes), 1) // width
    fold_w[...] = jnp.where(same, -1.5 * wide, 0.0)

    def chunk(c, carry):
        def one(g, carry):
            for i, block in enumerate(transform(c, g * group)):
                send[c, peer(g * group + i)] = block
                block_copy(c, g * group + i).start()
            return carry

        lax.fori_loop(0, n // group - 1, one, 0)
        last = n - group
        for i, block in enumerate(transform(c, last)):
            if i < group - 1:
                send[c, peer(last + i)] = block
                block_copy(c, last + i).start()
            else:
                recv[c, me] = block
        return carry

    lax.fori_loop(0, chunks, chunk, 0)

    pltpu.make_async_copy(
        dens_all.at[pl.ds(0, n - 1)], dens_all.at[pl.ds(0, n - 1)], drecv_sem
    ).wait()
    bra = iota((states, pairs), 0) == pair_ref[0:1, :]
    ket = iota((states, pairs), 0) == pair_ref[1:2, :]
    counts = jnp.broadcast_to(count_ref[...].astype(jnp.float32), (8, states)).astype(jnp.bfloat16)
    bra_count = lax.dot_general(
        counts, bra.astype(jnp.float32).astype(jnp.bfloat16), NN, preferred_element_type=jnp.float32
    )
    ket_count = lax.dot_general(
        counts, ket.astype(jnp.float32).astype(jnp.bfloat16), NN, preferred_element_type=jnp.float32
    )
    live_row = jnp.minimum(bra_count, ket_count)[0:1, :]
    row = iota((rows_p, pairs), 0)
    place = (lax.rem(row, 16) < own) & (row // 16 * own + lax.rem(row, 16) == iota((rows_p, pairs), 1))
    live = jnp.sum(jnp.where(place, live_row, 0.0), axis=1, keepdims=True).astype(jnp.int32)
    cell = iota((rows_p, cells), 1)
    inside = (cell // width < live) & (lax.rem(cell, width) < live)
    dmat[...] = jnp.where(inside, dens_all[...].astype(jnp.float32).reshape(rows_p, cells), 0.0)

    total = []
    for c in range(chunks):
        block = recv.at[c, pl.ds(0, n - 1)]
        pltpu.make_async_copy(block, block, recv_sem.at[c]).wait()
        summed = recv[c, 0]
        for s in range(1, n):
            summed = summed + recv[c, s]
        total.append(summed)

    cou_t = jnp.concatenate([t[:, 3 * lanes:] for t in total], axis=0)
    fit_in = cou_t * jnp.concatenate([fit_w[...]] * chunks, axis=0)
    fit_in = jnp.broadcast_to(
        jnp.sum(fit_in.reshape(chunks, width, lanes), axis=1, keepdims=True), (chunks, width, lanes)
    ).reshape(chunks * width, lanes)
    fitted = exact_dot(fit_in, same.astype(jnp.float32), NN)
    down = iota((chunks * width, lanes), 0)
    across = iota((chunks * width, lanes), 1)
    diagonal = lax.rem(down, width) == lax.rem(across, width)
    mixed = dot(cou_t, fold_w[...], NT) + jnp.where(diagonal, fitted, 0.0)
    stacked = jnp.concatenate(
        [t[:, 3 * width * p: 3 * width * (p + 1)] for t in total for p in range(k)], axis=0
    )
    mixed = jnp.concatenate([mixed[c * width:(c + 1) * width] for c in range(chunks)], axis=1)
    field = dot(mixed, stacked, NN) * scale

    deep = 3 * width
    laid = jnp.concatenate([p.astype(jnp.float32) for p in parts_of(field)], axis=1)
    laid = jnp.concatenate([laid] * width, axis=0)
    keep = iota((cells, 3 * deep), 0) // width == lax.rem(iota((cells, 3 * deep), 1), width)
    laid = jnp.where(keep, laid, 0.0).astype(jnp.bfloat16)
    pick = lax.rem(iota((8, 3 * deep), 1), deep) // width == iota((8, 3 * deep), 0)
    flat = lax.dot_general(
        pick.astype(jnp.float32).astype(jnp.bfloat16), laid, NT, preferred_element_type=jnp.float32
    )
    value = exact_dot(flat, dmat[...], NT)

    part_a[me] = value

    def a_copy(d):
        return pltpu.make_async_remote_copy(
            src_ref=part_a.at[me], dst_ref=part_a.at[me], send_sem=asend_sem, recv_sem=arecv_sem,
            device_id=(z, peer(d)), device_id_type=MESH,
        )

    for d in range(n - 1):
        a_copy(d).start()
    block = part_a.at[pl.ds(0, n - 1)]
    pltpu.make_async_copy(block, block, arecv_sem).wait()
    value = part_a[0]
    for s in range(1, n):
        value = value + part_a[s]

    part_b[z] = value

    def b_copy(d):
        return pltpu.make_async_remote_copy(
            src_ref=part_b.at[z], dst_ref=part_b.at[z], send_sem=bsend_sem, recv_sem=brecv_sem,
            device_id=(lax.rem(z + 1 + d, m), me), device_id_type=MESH,
        )

    for d in range(m - 1):
        b_copy(d).start()
    block = part_b.at[pl.ds(0, m - 1)]
    pltpu.make_async_copy(block, block, brecv_sem).wait()
    value = part_b[0]
    for s in range(1, m):
        value = value + part_b[s]

    slots = owner_ref.shape[1]
    row = iota((rows_p, slots), 0)
    chosen = (lax.rem(row, 16) < own) & (row // 16 * own + lax.rem(row, 16) == owner_ref[...])
    out_ref[...] = exact_dot(value, chosen.astype(jnp.float32), NN)[0:3, :]

    pltpu.make_async_copy(
        dens_all.at[pl.ds(0, n - 1)], dens_all.at[pl.ds(0, n - 1)], dsend_sem
    ).wait()
    for c in range(chunks):
        block = send.at[c, pl.ds(0, n - 1)]
        pltpu.make_async_copy(block, block, send_sem.at[c]).wait()
    block = part_a.at[pl.ds(0, n - 1)]
    pltpu.make_async_copy(block, block, asend_sem).wait()
    block = part_b.at[pl.ds(0, m - 1)]
    pltpu.make_async_copy(block, block, bsend_sem).wait()


def on_device(n, m, soc_ints, cou_ints, coef_t, active_rdm, spin_dens, pair_list, owner_map, state_count):
    slab, parts, width, span = soc_ints.shape
    k = max(1, slab // (n * 4))
    chunks = slab // (n * k)
    block = (parts + 1) * width * k
    own, cells = spin_dens.shape
    rows_p = n * 16
    scale = 1.0 / (8.0 * float(slab * m) ** 0.5 * width)
    vmem = pl.BlockSpec(memory_space=pltpu.VMEM)
    hbm = pl.BlockSpec(memory_space=pl.ANY)
    dma = pltpu.SemaphoreType.DMA
    return pl.pallas_call(
        functools.partial(kernel, n, m, chunks, k, 4, scale),
        out_shape=jax.ShapeDtypeStruct((parts, owner_map.shape[0]), jnp.float32),
        in_specs=[hbm] * 8,
        out_specs=vmem,
        scratch_shapes=[
            pltpu.VMEM((width, span), jnp.bfloat16),
            pltpu.VMEM((width, width), jnp.float32),
            pltpu.VMEM((own, cells), jnp.bfloat16),
            pltpu.VMEM((2, pair_list.shape[0]), jnp.int32),
            pltpu.VMEM((1, own), jnp.int32),
            pltpu.VMEM((1, state_count.shape[0]), jnp.int32),
            dma((6,)),
            pltpu.VMEM((slab, parts * width, span), jnp.bfloat16),
            pltpu.VMEM((slab, width, span), jnp.bfloat16),
            pltpu.VMEM((chunks, n, width, block), jnp.float32),
            pltpu.VMEM((chunks, n, width, block), jnp.float32),
            pltpu.VMEM((16, cells), jnp.bfloat16),
            pltpu.VMEM((n, 16, cells), jnp.bfloat16),
            pltpu.VMEM((rows_p, cells), jnp.float32),
            pltpu.VMEM((width, width * k), jnp.float32),
            pltpu.VMEM((width * k, width * k), jnp.float32),
            pltpu.VMEM((n, 8, rows_p), jnp.float32),
            pltpu.VMEM((m, 8, rows_p), jnp.float32),
            dma((chunks, n)), dma((chunks, n)), dma((chunks,)), dma((chunks,)),
            dma, dma, dma, dma, dma, dma,
        ],
        compiler_params=pltpu.CompilerParams(
            collective_id=0, has_side_effects=True, vmem_limit_bytes=60 * 1024 * 1024
        ),
        cost_estimate=pl.CostEstimate(
            flops=2 * slab * 4 * width * width * span, bytes_accessed=slab * 4 * width * span * 2,
            transcendentals=0,
        ),
    )(
        soc_ints.reshape(slab, parts * width, span), cou_ints, coef_t, active_rdm, spin_dens,
        pair_list.T, owner_map.reshape(1, -1), state_count.reshape(1, -1),
    )


def solution(mesh):
    return jax.shard_map(
        functools.partial(on_device, mesh.shape["ao"], mesh.shape["aux"]),
        mesh=mesh,
        in_specs=(
            P("aux", None, None, "ao"),
            P("aux", None, "ao"),
            P(None, "ao"),
            P(),
            P("ao", None),
            P(),
            P("ao"),
            P(),
        ),
        out_specs=P(None, "ao"),
        check_vma=False,
    )
```

```python
import functools

import jax
import jax.numpy as jnp
from jax import lax
from jax.experimental import pallas as pl
from jax.experimental.pallas import tpu as pltpu
from jax.sharding import PartitionSpec as P

MESH = pl.DeviceIdType.MESH
HIGH = lax.Precision.HIGHEST
NN = (((1,), (0,)), ((), ()))
NT = (((1,), (1,)), ((), ()))


def iota(shape, dim):
    return lax.broadcasted_iota(jnp.int32, shape, dim)


def dot(a, b, dims):
    return lax.dot_general(a, b, dims, precision=HIGH, preferred_element_type=jnp.float32)


def parts_of(x):
    hi = x.astype(jnp.bfloat16)
    rest = x - hi.astype(jnp.float32)
    mid = rest.astype(jnp.bfloat16)
    return hi, mid, (rest - mid.astype(jnp.float32)).astype(jnp.bfloat16)


def exact_dot(x, table, dims):
    rows = x.shape[0]
    stack = jnp.concatenate([p.astype(jnp.float32) for p in parts_of(x)], axis=0).astype(jnp.bfloat16)
    out = lax.dot_general(stack, table.astype(jnp.bfloat16), dims, preferred_element_type=jnp.float32)
    return out[:rows] + out[rows:2 * rows] + out[2 * rows:3 * rows]


def kernel(
    n, m, chunks, k, group, scale,
    soc_ref, cou_ref, coef_hbm, rdm_hbm, dens_hbm, pair_hbm, owner_hbm, count_hbm,
    out_ref,
    coef_ref, rdm_ref, dens_ref, pair_ref, owner_ref, count_ref, small_sem,
    soc_v, cou_v, sib_send, sib_recv, mine, recv, dens_out, dens_all, dmat, fit_w, fold_w,
    part_a, part_b,
    soc_sem, cou_sem, sib_ssem, sib_rsem, send_sem, recv_sem, dsend_sem, drecv_sem,
    asend_sem, arecv_sem, bsend_sem, brecv_sem,
):
    width = rdm_ref.shape[0]
    own = dens_ref.shape[0]
    cells = width * width
    states = count_ref.shape[1]
    pairs = pair_ref.shape[1]
    rows_p = n * 16
    me = lax.axis_index("ao")
    z = lax.axis_index("aux")
    q = n // 2
    my_chip = me // 2
    core = lax.rem(me, 2)
    sibling = my_chip * 2 + 1 - core

    def peer(d):
        chip = lax.rem(my_chip + 1 + lax.rem(d, q), q)
        return chip * 2 + lax.rem(me + 1 + d // q, 2)

    def fetch(c, d):
        at = (c * n + peer(d)) * k
        return (
            pltpu.make_async_copy(soc_ref.at[pl.ds(at, k)], soc_v.at[pl.ds(at, k)], soc_sem.at[c, d]),
            pltpu.make_async_copy(cou_ref.at[pl.ds(at, k)], cou_v.at[pl.ds(at, k)], cou_sem.at[c, d]),
        )

    def start_fetch(i, carry):
        for copy in fetch(i // n, lax.rem(i, n)):
            copy.start()
        return carry

    lax.fori_loop(0, group, start_fetch, 0)
    small = [
        pltpu.make_async_copy(a, b, small_sem.at[i])
        for i, (a, b) in enumerate([
            (coef_hbm, coef_ref), (rdm_hbm, rdm_ref), (dens_hbm, dens_ref),
            (pair_hbm, pair_ref), (owner_hbm, owner_ref), (count_hbm, count_ref),
        ])
    ]
    for copy in small:
        copy.start()

    barrier = pltpu.get_barrier_semaphore()
    for d in range(n - 1):
        pl.semaphore_signal(barrier, inc=1, device_id=(z, peer(d)), device_id_type=MESH)
    for d in range(m - 1):
        pl.semaphore_signal(
            barrier, inc=1, device_id=(lax.rem(z + 1 + d, m), me), device_id_type=MESH
        )

    lax.fori_loop(group, chunks * n, start_fetch, 0)
    for copy in small:
        copy.wait()

    dens = dens_ref[...].astype(jnp.float32)
    if own < 16:
        dens = jnp.concatenate([dens, jnp.zeros((16 - own, cells), jnp.float32)], axis=0)
    dens_out[...] = dens.astype(jnp.bfloat16)
    dens_all[me] = dens.astype(jnp.bfloat16)

    pl.semaphore_wait(barrier, n + m - 2)

    def dens_copy(d):
        return pltpu.make_async_remote_copy(
            src_ref=dens_out, dst_ref=dens_all.at[me], send_sem=dsend_sem, recv_sem=drecv_sem,
            device_id=(z, peer(d)), device_id_type=MESH,
        )

    def sibling_copy(c):
        return pltpu.make_async_remote_copy(
            src_ref=sib_send.at[c], dst_ref=sib_recv.at[c],
            send_sem=sib_ssem.at[c], recv_sem=sib_rsem.at[c],
            device_id=(z, sibling), device_id_type=MESH,
        )

    def block_copy(c, chip):
        return pltpu.make_async_remote_copy(
            src_ref=mine.at[c, chip], dst_ref=recv.at[c, my_chip],
            send_sem=send_sem.at[c], recv_sem=recv_sem.at[c],
            device_id=(z, chip * 2 + core), device_id_type=MESH,
        )

    span = soc_v.shape[-1]
    block_rows = 4 * width * k

    def transform(c, first):
        for i in range(group):
            for copy in fetch(c, first + i):
                copy.wait()
        rows = []
        for i in range(group):
            at = (c * n + peer(first + i)) * k
            rows.append(soc_v[pl.ds(at, k)].reshape(3 * width * k, span))
            rows.append(cou_v[pl.ds(at, k)].reshape(width * k, span))
        out = lax.dot_general(
            coef_ref[...], jnp.concatenate(rows, axis=0), NT, preferred_element_type=jnp.float32
        )
        return [out[:, i * block_rows:(i + 1) * block_rows] for i in range(group)]

    for d in range(n - 1):
        dens_copy(d).start()

    lanes = width * k
    rdm = rdm_ref[...]
    spread = (lax.rem(iota((width, lanes), 1), width) == iota((width, lanes), 0)).astype(jnp.float32)
    tiled = jnp.concatenate([rdm] * k, axis=0)
    eye = (iota((width, width), 0) == iota((width, width), 1)).astype(jnp.float32)
    fit_w[...] = dot(eye, tiled, NT)
    wide = dot(rdm, spread, NN)
    wide = jnp.concatenate([wide] * k, axis=0)
    same = iota((lanes, lanes), 0) // width == iota((lanes, lanes), 1) // width
    fold_w[...] = jnp.where(same, -1.5 * wide, 0.0)

    def half(c, first, target):
        for g in range(q // group):
            at = first + g * group
            for i, block in enumerate(transform(c, at)):
                target[c, lax.rem(my_chip + 1 + g * group + i, q)] = block

    def forward(c):
        sibling_copy(c).wait_recv()
        for i in range(q - 1):
            chip = lax.rem(my_chip + 1 + i, q)
            mine[c, chip] = mine[c, chip] + sib_recv[c, chip]
            block_copy(c, chip).start()
        recv[c, my_chip] = mine[c, my_chip] + sib_recv[c, my_chip]

    half(0, 0, sib_send)
    sibling_copy(0).start()
    half(0, q, mine)

    def chunk(c, carry):
        half(c, 0, sib_send)
        sibling_copy(c).start()
        forward(c - 1)
        half(c, q, mine)
        return carry

    lax.fori_loop(1, chunks, chunk, 0)
    forward(chunks - 1)

    pltpu.make_async_copy(
        dens_all.at[pl.ds(0, n - 1)], dens_all.at[pl.ds(0, n - 1)], drecv_sem
    ).wait()
    bra = iota((states, pairs), 0) == pair_ref[0:1, :]
    ket = iota((states, pairs), 0) == pair_ref[1:2, :]
    counts = jnp.broadcast_to(count_ref[...].astype(jnp.float32), (8, states)).astype(jnp.bfloat16)
    bra_count = lax.dot_general(
        counts, bra.astype(jnp.float32).astype(jnp.bfloat16), NN, preferred_element_type=jnp.float32
    )
    ket_count = lax.dot_general(
        counts, ket.astype(jnp.float32).astype(jnp.bfloat16), NN, preferred_element_type=jnp.float32
    )
    live_row = jnp.minimum(bra_count, ket_count)[0:1, :]
    row = iota((rows_p, pairs), 0)
    place = (lax.rem(row, 16) < own) & (row // 16 * own + lax.rem(row, 16) == iota((rows_p, pairs), 1))
    live = jnp.sum(jnp.where(place, live_row, 0.0), axis=1, keepdims=True).astype(jnp.int32)
    cell = iota((rows_p, cells), 1)
    inside = (cell // width < live) & (lax.rem(cell, width) < live)
    dmat[...] = jnp.where(inside, dens_all[...].astype(jnp.float32).reshape(rows_p, cells), 0.0)

    total = []
    for c in range(chunks):
        block = recv.at[c, pl.ds(0, q - 1)]
        pltpu.make_async_copy(block, block, recv_sem.at[c]).wait()
        summed = recv[c, 0]
        for s in range(1, q):
            summed = summed + recv[c, s]
        total.append(summed)

    cou_t = jnp.concatenate([t[:, 3 * lanes:] for t in total], axis=0)
    fit_in = cou_t * jnp.concatenate([fit_w[...]] * chunks, axis=0)
    fit_in = jnp.broadcast_to(
        jnp.sum(fit_in.reshape(chunks, width, lanes), axis=1, keepdims=True), (chunks, width, lanes)
    ).reshape(chunks * width, lanes)
    fitted = exact_dot(fit_in, same.astype(jnp.float32), NN)
    down = iota((chunks * width, lanes), 0)
    across = iota((chunks * width, lanes), 1)
    diagonal = lax.rem(down, width) == lax.rem(across, width)
    mixed = dot(cou_t, fold_w[...], NT) + jnp.where(diagonal, fitted, 0.0)
    stacked = jnp.concatenate(
        [t[:, 3 * width * p: 3 * width * (p + 1)] for t in total for p in range(k)], axis=0
    )
    mixed = jnp.concatenate([mixed[c * width:(c + 1) * width] for c in range(chunks)], axis=1)
    field = dot(mixed, stacked, NN) * scale

    deep = 3 * width
    laid = jnp.concatenate([p.astype(jnp.float32) for p in parts_of(field)], axis=1)
    laid = jnp.concatenate([laid] * width, axis=0)
    keep = iota((cells, 3 * deep), 0) // width == lax.rem(iota((cells, 3 * deep), 1), width)
    laid = jnp.where(keep, laid, 0.0).astype(jnp.bfloat16)
    pick = lax.rem(iota((8, 3 * deep), 1), deep) // width == iota((8, 3 * deep), 0)
    flat = lax.dot_general(
        pick.astype(jnp.float32).astype(jnp.bfloat16), laid, NT, preferred_element_type=jnp.float32
    )
    value = exact_dot(flat, dmat[...], NT)

    part_a[me] = value

    def a_copy(d):
        return pltpu.make_async_remote_copy(
            src_ref=part_a.at[me], dst_ref=part_a.at[me], send_sem=asend_sem, recv_sem=arecv_sem,
            device_id=(z, peer(d)), device_id_type=MESH,
        )

    for d in range(n - 1):
        a_copy(d).start()
    block = part_a.at[pl.ds(0, n - 1)]
    pltpu.make_async_copy(block, block, arecv_sem).wait()
    value = part_a[0]
    for s in range(1, n):
        value = value + part_a[s]

    part_b[z] = value

    def b_copy(d):
        return pltpu.make_async_remote_copy(
            src_ref=part_b.at[z], dst_ref=part_b.at[z], send_sem=bsend_sem, recv_sem=brecv_sem,
            device_id=(lax.rem(z + 1 + d, m), me), device_id_type=MESH,
        )

    for d in range(m - 1):
        b_copy(d).start()
    block = part_b.at[pl.ds(0, m - 1)]
    pltpu.make_async_copy(block, block, brecv_sem).wait()
    value = part_b[0]
    for s in range(1, m):
        value = value + part_b[s]

    slots = owner_ref.shape[1]
    row = iota((rows_p, slots), 0)
    chosen = (lax.rem(row, 16) < own) & (row // 16 * own + lax.rem(row, 16) == owner_ref[...])
    out_ref[...] = exact_dot(value, chosen.astype(jnp.float32), NN)[0:3, :]

    pltpu.make_async_copy(
        dens_all.at[pl.ds(0, n - 1)], dens_all.at[pl.ds(0, n - 1)], dsend_sem
    ).wait()
    for c in range(chunks):
        sibling_copy(c).wait_send()
        block = mine.at[c, pl.ds(0, q - 1)]
        pltpu.make_async_copy(block, block, send_sem.at[c]).wait()
    block = part_a.at[pl.ds(0, n - 1)]
    pltpu.make_async_copy(block, block, asend_sem).wait()
    block = part_b.at[pl.ds(0, m - 1)]
    pltpu.make_async_copy(block, block, bsend_sem).wait()


def on_device(n, m, soc_ints, cou_ints, coef_t, active_rdm, spin_dens, pair_list, owner_map, state_count):
    slab, parts, width, span = soc_ints.shape
    k = max(1, slab // (n * 4))
    chunks = slab // (n * k)
    block = (parts + 1) * width * k
    own, cells = spin_dens.shape
    rows_p = n * 16
    scale = 1.0 / (8.0 * float(slab * m) ** 0.5 * width)
    vmem = pl.BlockSpec(memory_space=pltpu.VMEM)
    hbm = pl.BlockSpec(memory_space=pl.ANY)
    dma = pltpu.SemaphoreType.DMA
    return pl.pallas_call(
        functools.partial(kernel, n, m, chunks, k, 4, scale),
        out_shape=jax.ShapeDtypeStruct((parts, owner_map.shape[0]), jnp.float32),
        in_specs=[hbm] * 8,
        out_specs=vmem,
        scratch_shapes=[
            pltpu.VMEM((width, span), jnp.bfloat16),
            pltpu.VMEM((width, width), jnp.float32),
            pltpu.VMEM((own, cells), jnp.bfloat16),
            pltpu.VMEM((2, pair_list.shape[0]), jnp.int32),
            pltpu.VMEM((1, own), jnp.int32),
            pltpu.VMEM((1, state_count.shape[0]), jnp.int32),
            dma((6,)),
            pltpu.VMEM((slab, parts * width, span), jnp.bfloat16),
            pltpu.VMEM((slab, width, span), jnp.bfloat16),
            pltpu.VMEM((chunks, n // 2, width, block), jnp.float32),
            pltpu.VMEM((chunks, n // 2, width, block), jnp.float32),
            pltpu.VMEM((chunks, n // 2, width, block), jnp.float32),
            pltpu.VMEM((chunks, n // 2, width, block), jnp.float32),
            pltpu.VMEM((16, cells), jnp.bfloat16),
            pltpu.VMEM((n, 16, cells), jnp.bfloat16),
            pltpu.VMEM((rows_p, cells), jnp.float32),
            pltpu.VMEM((width, width * k), jnp.float32),
            pltpu.VMEM((width * k, width * k), jnp.float32),
            pltpu.VMEM((n, 8, rows_p), jnp.float32),
            pltpu.VMEM((m, 8, rows_p), jnp.float32),
            dma((chunks, n)), dma((chunks, n)), dma((chunks,)), dma((chunks,)), dma((chunks,)), dma((chunks,)),
            dma, dma, dma, dma, dma, dma,
        ],
        compiler_params=pltpu.CompilerParams(
            collective_id=0, has_side_effects=True, vmem_limit_bytes=60 * 1024 * 1024
        ),
        cost_estimate=pl.CostEstimate(
            flops=2 * slab * 4 * width * width * span, bytes_accessed=slab * 4 * width * span * 2,
            transcendentals=0,
        ),
    )(
        soc_ints.reshape(slab, parts * width, span), cou_ints, coef_t, active_rdm, spin_dens,
        pair_list.T, owner_map.reshape(1, -1), state_count.reshape(1, -1),
    )


def solution(mesh):
    return jax.shard_map(
        functools.partial(on_device, mesh.shape["ao"], mesh.shape["aux"]),
        mesh=mesh,
        in_specs=(
            P("aux", None, None, "ao"),
            P("aux", None, "ao"),
            P(None, "ao"),
            P(),
            P("ao", None),
            P(),
            P("ao"),
            P(),
        ),
        out_specs=P(None, "ao"),
        check_vma=False,
    )
```

```python
import functools

import jax
import jax.numpy as jnp
from jax import lax
from jax.experimental import pallas as pl
from jax.experimental.pallas import tpu as pltpu
from jax.sharding import PartitionSpec as P

MESH = pl.DeviceIdType.MESH
HIGH = lax.Precision.HIGHEST
NN = (((1,), (0,)), ((), ()))
NT = (((1,), (1,)), ((), ()))


def iota(shape, dim):
    return lax.broadcasted_iota(jnp.int32, shape, dim)


def dot(a, b, dims):
    return lax.dot_general(a, b, dims, precision=HIGH, preferred_element_type=jnp.float32)


def parts_of(x):
    hi = x.astype(jnp.bfloat16)
    rest = x - hi.astype(jnp.float32)
    mid = rest.astype(jnp.bfloat16)
    return hi, mid, (rest - mid.astype(jnp.float32)).astype(jnp.bfloat16)


def exact_dot(x, table, dims):
    rows = x.shape[0]
    stack = jnp.concatenate([p.astype(jnp.float32) for p in parts_of(x)], axis=0).astype(jnp.bfloat16)
    out = lax.dot_general(stack, table.astype(jnp.bfloat16), dims, preferred_element_type=jnp.float32)
    return out[:rows] + out[rows:2 * rows] + out[2 * rows:3 * rows]


def kernel(
    n, m, chunks, k, group, scale,
    soc_ref, cou_ref, coef_hbm, rdm_hbm, dens_hbm, pair_hbm, owner_hbm, count_hbm,
    out_ref,
    coef_ref, rdm_ref, dens_ref, pair_ref, owner_ref, count_ref, small_sem,
    soc_v, cou_v, send, recv, dens_out, dens_all, dmat, fit_w, fold_w,
    part_a, part_b,
    soc_sem, cou_sem, send_sem, recv_sem, dsend_sem, drecv_sem,
    asend_sem, arecv_sem, bsend_sem, brecv_sem,
):
    width = rdm_ref.shape[0]
    own = dens_ref.shape[0]
    cells = width * width
    states = count_ref.shape[1]
    pairs = pair_ref.shape[1]
    rows_p = n * 16
    me = lax.axis_index("ao")
    z = lax.axis_index("aux")

    def peer(d):
        chip = lax.rem(me // 2 + 1 + d // 2, n // 2)
        return chip * 2 + lax.rem(me + 1 + d, 2)

    def fetch(c):
        part = pl.ds(c * n * k, n * k)
        return (
            pltpu.make_async_copy(soc_ref.at[part], soc_v.at[part], soc_sem.at[c]),
            pltpu.make_async_copy(cou_ref.at[part], cou_v.at[part], cou_sem.at[c]),
        )

    for copy in fetch(0):
        copy.start()
    small = [
        pltpu.make_async_copy(a, b, small_sem.at[i])
        for i, (a, b) in enumerate([
            (coef_hbm, coef_ref), (rdm_hbm, rdm_ref), (dens_hbm, dens_ref),
            (pair_hbm, pair_ref), (owner_hbm, owner_ref), (count_hbm, count_ref),
        ])
    ]
    for copy in small:
        copy.start()

    barrier = pltpu.get_barrier_semaphore()
    for d in range(n - 1):
        pl.semaphore_signal(barrier, inc=1, device_id=(z, peer(d)), device_id_type=MESH)
    for d in range(m - 1):
        pl.semaphore_signal(
            barrier, inc=1, device_id=(lax.rem(z + 1 + d, m), me), device_id_type=MESH
        )

    for c in range(1, chunks):
        for copy in fetch(c):
            copy.start()
    for copy in small:
        copy.wait()

    dens = dens_ref[...].astype(jnp.float32)
    if own < 16:
        dens = jnp.concatenate([dens, jnp.zeros((16 - own, cells), jnp.float32)], axis=0)
    dens_out[...] = dens.astype(jnp.bfloat16)
    dens_all[me] = dens.astype(jnp.bfloat16)

    pl.semaphore_wait(barrier, n + m - 2)

    def dens_copy(d):
        return pltpu.make_async_remote_copy(
            src_ref=dens_out, dst_ref=dens_all.at[me], send_sem=dsend_sem, recv_sem=drecv_sem,
            device_id=(z, peer(d)), device_id_type=MESH,
        )

    def block_copy(c, d):
        j = peer(d)
        return pltpu.make_async_remote_copy(
            src_ref=send.at[c, j], dst_ref=recv.at[c, me],
            send_sem=send_sem.at[c], recv_sem=recv_sem.at[c],
            device_id=(z, j), device_id_type=MESH,
        )

    span = soc_v.shape[-1]
    block_rows = 4 * width * k

    def transform(c, first):
        rows = []
        for i in range(group):
            at = (c * n + peer(first + i)) * k
            rows.append(soc_v[pl.ds(at, k)].reshape(3 * width * k, span))
            rows.append(cou_v[pl.ds(at, k)].reshape(width * k, span))
        out = lax.dot_general(
            coef_ref[...], jnp.concatenate(rows, axis=0), NT, preferred_element_type=jnp.float32
        )
        return [out[:, i * block_rows:(i + 1) * block_rows] for i in range(group)]

    for d in range(n - 1):
        dens_copy(d).start()

    lanes = width * k
    rdm = rdm_ref[...]
    spread = (lax.rem(iota((width, lanes), 1), width) == iota((width, lanes), 0)).astype(jnp.float32)
    tiled = jnp.concatenate([rdm] * k, axis=0)
    eye = (iota((width, width), 0) == iota((width, width), 1)).astype(jnp.float32)
    fit_w[...] = dot(eye, tiled, NT)
    wide = dot(rdm, spread, NN)
    wide = jnp.concatenate([wide] * k, axis=0)
    same = iota((lanes, lanes), 0) // width == iota((lanes, lanes), 1) // width
    fold_w[...] = jnp.where(same, -1.5 * wide, 0.0)

    def chunk(c, carry):
        for copy in fetch(c):
            copy.wait()

        def one(g, carry):
            for i, block in enumerate(transform(c, g * group)):
                send[c, peer(g * group + i)] = block
                block_copy(c, g * group + i).start()
            return carry

        lax.fori_loop(0, n // group - 1, one, 0)
        last = n - group
        for i, block in enumerate(transform(c, last)):
            if i < group - 1:
                send[c, peer(last + i)] = block
                block_copy(c, last + i).start()
            else:
                recv[c, me] = block
        return carry

    lax.fori_loop(0, chunks, chunk, 0)

    pltpu.make_async_copy(
        dens_all.at[pl.ds(0, n - 1)], dens_all.at[pl.ds(0, n - 1)], drecv_sem
    ).wait()
    bra = iota((states, pairs), 0) == pair_ref[0:1, :]
    ket = iota((states, pairs), 0) == pair_ref[1:2, :]
    counts = jnp.broadcast_to(count_ref[...].astype(jnp.float32), (8, states)).astype(jnp.bfloat16)
    bra_count = lax.dot_general(
        counts, bra.astype(jnp.float32).astype(jnp.bfloat16), NN, preferred_element_type=jnp.float32
    )
    ket_count = lax.dot_general(
        counts, ket.astype(jnp.float32).astype(jnp.bfloat16), NN, preferred_element_type=jnp.float32
    )
    live_row = jnp.minimum(bra_count, ket_count)[0:1, :]
    row = iota((rows_p, pairs), 0)
    place = (lax.rem(row, 16) < own) & (row // 16 * own + lax.rem(row, 16) == iota((rows_p, pairs), 1))
    live = jnp.sum(jnp.where(place, live_row, 0.0), axis=1, keepdims=True).astype(jnp.int32)
    cell = iota((rows_p, cells), 1)
    inside = (cell // width < live) & (lax.rem(cell, width) < live)
    dmat[...] = jnp.where(inside, dens_all[...].astype(jnp.float32).reshape(rows_p, cells), 0.0)

    total = []
    for c in range(chunks):
        block = recv.at[c, pl.ds(0, n - 1)]
        pltpu.make_async_copy(block, block, recv_sem.at[c]).wait()
        summed = recv[c, 0]
        for s in range(1, n):
            summed = summed + recv[c, s]
        total.append(summed)

    cou_t = jnp.concatenate([t[:, 3 * lanes:] for t in total], axis=0)
    fit_in = cou_t * jnp.concatenate([fit_w[...]] * chunks, axis=0)
    fit_in = jnp.broadcast_to(
        jnp.sum(fit_in.reshape(chunks, width, lanes), axis=1, keepdims=True), (chunks, width, lanes)
    ).reshape(chunks * width, lanes)
    fitted = exact_dot(fit_in, same.astype(jnp.float32), NN)
    down = iota((chunks * width, lanes), 0)
    across = iota((chunks * width, lanes), 1)
    diagonal = lax.rem(down, width) == lax.rem(across, width)
    mixed = dot(cou_t, fold_w[...], NT) + jnp.where(diagonal, fitted, 0.0)
    stacked = jnp.concatenate(
        [t[:, 3 * width * p: 3 * width * (p + 1)] for t in total for p in range(k)], axis=0
    )
    mixed = jnp.concatenate([mixed[c * width:(c + 1) * width] for c in range(chunks)], axis=1)
    field = dot(mixed, stacked, NN) * scale

    deep = 3 * width
    laid = jnp.concatenate([p.astype(jnp.float32) for p in parts_of(field)], axis=1)
    laid = jnp.concatenate([laid] * width, axis=0)
    keep = iota((cells, 3 * deep), 0) // width == lax.rem(iota((cells, 3 * deep), 1), width)
    laid = jnp.where(keep, laid, 0.0).astype(jnp.bfloat16)
    pick = lax.rem(iota((8, 3 * deep), 1), deep) // width == iota((8, 3 * deep), 0)
    flat = lax.dot_general(
        pick.astype(jnp.float32).astype(jnp.bfloat16), laid, NT, preferred_element_type=jnp.float32
    )
    value = exact_dot(flat, dmat[...], NT)

    part_a[me] = value

    def a_copy(d):
        return pltpu.make_async_remote_copy(
            src_ref=part_a.at[me], dst_ref=part_a.at[me], send_sem=asend_sem, recv_sem=arecv_sem,
            device_id=(z, peer(d)), device_id_type=MESH,
        )

    for d in range(n - 1):
        a_copy(d).start()
    block = part_a.at[pl.ds(0, n - 1)]
    pltpu.make_async_copy(block, block, arecv_sem).wait()
    value = part_a[0]
    for s in range(1, n):
        value = value + part_a[s]

    part_b[z] = value

    def b_copy(d):
        return pltpu.make_async_remote_copy(
            src_ref=part_b.at[z], dst_ref=part_b.at[z], send_sem=bsend_sem, recv_sem=brecv_sem,
            device_id=(lax.rem(z + 1 + d, m), me), device_id_type=MESH,
        )

    for d in range(m - 1):
        b_copy(d).start()
    block = part_b.at[pl.ds(0, m - 1)]
    pltpu.make_async_copy(block, block, brecv_sem).wait()
    value = part_b[0]
    for s in range(1, m):
        value = value + part_b[s]

    slots = owner_ref.shape[1]
    row = iota((rows_p, slots), 0)
    chosen = (lax.rem(row, 16) < own) & (row // 16 * own + lax.rem(row, 16) == owner_ref[...])
    out_ref[...] = exact_dot(value, chosen.astype(jnp.float32), NN)[0:3, :]

    pltpu.make_async_copy(
        dens_all.at[pl.ds(0, n - 1)], dens_all.at[pl.ds(0, n - 1)], dsend_sem
    ).wait()
    for c in range(chunks):
        block = send.at[c, pl.ds(0, n - 1)]
        pltpu.make_async_copy(block, block, send_sem.at[c]).wait()
    block = part_a.at[pl.ds(0, n - 1)]
    pltpu.make_async_copy(block, block, asend_sem).wait()
    block = part_b.at[pl.ds(0, m - 1)]
    pltpu.make_async_copy(block, block, bsend_sem).wait()


def on_device(n, m, soc_ints, cou_ints, coef_t, active_rdm, spin_dens, pair_list, owner_map, state_count):
    slab, parts, width, span = soc_ints.shape
    k = max(1, slab // (n * 4))
    chunks = slab // (n * k)
    block = (parts + 1) * width * k
    own, cells = spin_dens.shape
    rows_p = n * 16
    scale = 1.0 / (8.0 * float(slab * m) ** 0.5 * width)
    vmem = pl.BlockSpec(memory_space=pltpu.VMEM)
    hbm = pl.BlockSpec(memory_space=pl.ANY)
    dma = pltpu.SemaphoreType.DMA
    return pl.pallas_call(
        functools.partial(kernel, n, m, chunks, k, 4, scale),
        out_shape=jax.ShapeDtypeStruct((parts, owner_map.shape[0]), jnp.float32),
        in_specs=[hbm] * 8,
        out_specs=vmem,
        scratch_shapes=[
            pltpu.VMEM((width, span), jnp.bfloat16),
            pltpu.VMEM((width, width), jnp.float32),
            pltpu.VMEM((own, cells), jnp.bfloat16),
            pltpu.VMEM((2, pair_list.shape[0]), jnp.int32),
            pltpu.VMEM((1, own), jnp.int32),
            pltpu.VMEM((1, state_count.shape[0]), jnp.int32),
            dma((6,)),
            pltpu.VMEM((slab, parts * width, span), jnp.bfloat16),
            pltpu.VMEM((slab, width, span), jnp.bfloat16),
            pltpu.VMEM((chunks, n, width, block), jnp.float32),
            pltpu.VMEM((chunks, n, width, block), jnp.float32),
            pltpu.VMEM((16, cells), jnp.bfloat16),
            pltpu.VMEM((n, 16, cells), jnp.bfloat16),
            pltpu.VMEM((rows_p, cells), jnp.float32),
            pltpu.VMEM((width, width * k), jnp.float32),
            pltpu.VMEM((width * k, width * k), jnp.float32),
            pltpu.VMEM((n, 8, rows_p), jnp.float32),
            pltpu.VMEM((m, 8, rows_p), jnp.float32),
            dma((chunks,)), dma((chunks,)), dma((chunks,)), dma((chunks,)),
            dma, dma, dma, dma, dma, dma,
        ],
        compiler_params=pltpu.CompilerParams(
            collective_id=0, has_side_effects=True, vmem_limit_bytes=60 * 1024 * 1024
        ),
        cost_estimate=pl.CostEstimate(
            flops=2 * slab * 4 * width * width * span, bytes_accessed=slab * 4 * width * span * 2,
            transcendentals=0,
        ),
    )(
        soc_ints.reshape(slab, parts * width, span), cou_ints, coef_t, active_rdm, spin_dens,
        pair_list.T, owner_map.reshape(1, -1), state_count.reshape(1, -1),
    )


def solution(mesh):
    return jax.shard_map(
        functools.partial(on_device, mesh.shape["ao"], mesh.shape["aux"]),
        mesh=mesh,
        in_specs=(
            P("aux", None, None, "ao"),
            P("aux", None, "ao"),
            P(None, "ao"),
            P(),
            P("ao", None),
            P(),
            P("ao"),
            P(),
        ),
        out_specs=P(None, "ao"),
        check_vma=False,
    )
```
